32 devices in a mesh: tm: 2 (over x), gz: 4 (over y, core), view: 4 (over z).
Axes of the slice: x: 2, y: 2, z: 4, core: 2. Of those that a mesh axis runs over, the one named last changes fastest.
Arguments:
- sinogram: bfloat16 [2, 8, 512, 2560], P(None, 'view', ('tm', 'gz')), may hold values from 102 to 358
- projector: bfloat16 [8, 1024, 2560], P('view'), may hold values from 0.0099487305 to 1
- warm_volume: float32 [512, 1024], P(('tm', 'gz')), may hold values from 0.2 to 2.5, as said below
- view_order: int32 [2], replicated, may hold values from 0 to 1, each once
Outputs:
- volumes: float32 [2, 512, 1024], P(None, ('tm', 'gz'))
The draws below stay inside these ranges and needn't reach their ends.
Inputs may be any that keep to these rules, and one draw needn't show every extreme that they name: `view_order`: each local view number appears once. `warm_volume`: positive attenuation values.
All inputs are finite; a program needn't handle non-finite values.
Results may differ from the reference program's by a relative error of at most 0.0003.
Values may be sent and summed in bfloat16 or wider, within the bound.
A program may use at most 64 MiB of HBM per device.

```python
import math
import jax
import jax.numpy as jnp
from jax import lax

DET = 2560
RY = 128
PIX = 1024
VB = 2
FRAMES = 2
SWEEPS = 3
TV_STEPS = 2
NZ = 512
NV = 8
N_VIEW = 4


def draw_warm_volume(key, part):
    zpos = jnp.arange(NZ, dtype=jnp.float32) / max(NZ - 1, 1)
    amplitude = 0.15 * 3.0 ** zpos
    first_key = jax.random.fold_in(key, 0)
    noise = jax.random.uniform(first_key, (NZ, PIX), jnp.float32, minval=-1.0, maxval=1.0)
    return (1.0 + amplitude[:, None] * noise).astype(jnp.float32)


def shard_levels(rng, extent, cuts, smallest, largest):
    loudness = 1.0
    for dim, shards_of in cuts:
        steps = jax.random.uniform(jax.random.fold_in(jax.random.fold_in(rng, 6), dim), (shards_of,), jnp.float32, smallest / len(cuts), largest / len(cuts))
        loudness = loudness * jnp.repeat(jnp.exp(steps), extent[dim] // shards_of).reshape((-1,) + (1,) * (len(extent) - 1 - dim))
    return loudness


def setup_inputs(seed: int = 0) -> dict:
    streams_of = jax.random.split(jax.random.key(seed), 5)
    return {
        "sinogram": jnp.clip(102.0 + 256.0 * jax.random.uniform(streams_of[0], (FRAMES, NV, NZ, DET), jnp.float32) ** shard_levels(streams_of[0], (FRAMES, NV, NZ, DET), ((1, 4), (2, 8)), -0.2, 0.2), 102.0, 358.0).astype(jnp.bfloat16),
        "projector": jnp.clip(jnp.exp(math.log(1.0) - 4.61031033 * jax.random.uniform(streams_of[1], (NV, PIX, DET), jnp.float32) ** shard_levels(streams_of[1], (NV, PIX, DET), ((0, 4),), -0.2, 0.2)), 0.0099487305, 1.0).astype(jnp.bfloat16),
        "warm_volume": draw_warm_volume(jax.random.fold_in(streams_of[4], 71), 0),
        "view_order": jax.random.permutation(streams_of[3], VB).astype(jnp.int32),
    }


RELAXATION = 0.9
STEP_SCALE = 0.3
STEP_DECAY = 0.7
SMOOTHING = 0.01
NORM_GUARD = 1e-06

def tv_gradient(volume, first_z, depth_total):
    row_count = volume.shape[0]
    pixels = volume.shape[1]
    zero_row = jnp.zeros((1, pixels), jnp.float32)
    zero_band = jnp.zeros((row_count, RY), jnp.float32)
    zero_col = jnp.zeros((row_count, 1), jnp.float32)
    zindex = first_z + jnp.arange(row_count, dtype=jnp.int32)
    inside = ((zindex >= 0) & (zindex < depth_total - 1)).astype(jnp.float32)
    diff_z = jnp.concatenate([volume[1:] - volume[:-1], zero_row], axis=0) * inside[:, None]
    diff_i = jnp.concatenate([volume[:, RY:] - volume[:, :-RY], zero_band], axis=1)
    column = jnp.arange(pixels, dtype=jnp.int32) % RY
    diff_j = jnp.concatenate([volume[:, 1:] - volume[:, :-1], zero_col], axis=1)
    diff_j = diff_j * (column < RY - 1).astype(jnp.float32)[None, :]
    magnitude = jnp.sqrt(diff_z * diff_z + diff_i * diff_i + diff_j * diff_j + SMOOTHING)
    flux_z = diff_z / magnitude
    flux_i = diff_i / magnitude
    flux_j = diff_j / magnitude
    gradient = jnp.concatenate([zero_row, flux_z[:-1]], axis=0) - flux_z
    gradient = gradient + (jnp.concatenate([zero_band, flux_i[:, :-RY]], axis=1) - flux_i)
    gradient = gradient + (jnp.concatenate([zero_col, flux_j[:, :-1]], axis=1) - flux_j)
    return gradient

def superize(volume, first_step):
    for step_no in range(TV_STEPS):
        gradient = tv_gradient(volume, 0, NZ)
        spread = jnp.sqrt(jnp.sum(gradient * gradient) / (NZ * PIX) + NORM_GUARD)
        volume = volume - STEP_SCALE * STEP_DECAY ** (first_step + step_no) * gradient / spread
    return volume

def reference(sinogram, projector, warm_volume, view_order):
    tile_stack = projector.reshape(N_VIEW, VB, PIX, DET)
    ray_sums = lax.optimization_barrier(jnp.sum(tile_stack, axis=2, dtype=jnp.float32))
    coverage = lax.optimization_barrier(jnp.sum(tile_stack, axis=(0, 3), dtype=jnp.float32))
    frame_data = sinogram.reshape(FRAMES, N_VIEW, VB, NZ, DET)
    volume = warm_volume
    finished = []
    for frame_no in range(FRAMES):
        for sweep_no in range(SWEEPS):
            volume = superize(volume, sweep_no * TV_STEPS)
            for subset in range(VB):
                slot_index = view_order[subset]
                tiles = jnp.take(tile_stack, slot_index, axis=1)
                totals = jnp.take(ray_sums, slot_index, axis=1)
                observed = jnp.take(frame_data[frame_no], slot_index, axis=1)
                rounded = volume.astype(jnp.bfloat16)

                def backproject(items):
                    ray_tile, observed_rows, ray_total = items
                    forward = jnp.dot(rounded, ray_tile, preferred_element_type=jnp.float32)
                    mismatch = ((observed_rows.astype(jnp.float32) - forward) / ray_total[None, :]).astype(jnp.bfloat16)
                    return lax.dot_general(mismatch, ray_tile, (((1,), (1,)), ((), ())), preferred_element_type=jnp.float32)
                partial_back = lax.map(backproject, (tiles, observed, totals))
                summed = lax.optimization_barrier(jnp.sum(partial_back, axis=0))
                weight = jnp.take(coverage, slot_index, axis=0)
                volume = jnp.maximum(volume + RELAXATION * summed / weight[None, :], 0.0)
        finished.append(volume)
    return jnp.stack(finished, axis=0)
```

```python
import functools

import jax
import jax.numpy as jnp
from jax import lax
from jax.experimental import pallas as pl
from jax.experimental.pallas import tpu as pltpu
from jax.sharding import PartitionSpec as P

RY = 128
FRAMES = 2
SWEEPS = 3
TV_STEPS = 2
RELAXATION = 0.9
STEP_SCALE = 0.3
STEP_DECAY = 0.7
SMOOTHING = 0.01
NORM_GUARD = 1e-06
RIM = 8

MESH = pl.DeviceIdType.MESH


def slab_device(index, gz):
    return {"tm": lax.div(index, gz), "gz": lax.rem(index, gz)}


def iterate_kernel(
    slabs, gz, gram_ref, back_ref, cover_ref, warm_ref, out_ref,
    xs, grad, fluxz, defect, own, stat, rim, stat_send, stat_recv, rim_send, rim_recv,
):
    me = lax.axis_index("tm") * gz + lax.axis_index("gz")
    ext, pixels = warm_ref.shape
    rows = ext - 2 * RIM
    depth_total = slabs * rows
    per_view = gram_ref.shape[0]
    tiles = pixels // RY

    barrier = pltpu.get_barrier_semaphore()
    for d in range(1, slabs):
        pl.semaphore_signal(
            barrier, inc=1, device_id=slab_device(lax.rem(me + d, slabs), gz), device_id_type=MESH
        )

    xs[:ext] = warm_ref[...]
    xs[ext:] = jnp.zeros((8, pixels), jnp.float32)
    fluxz[:8] = jnp.zeros((8, pixels), jnp.float32)
    ones = jnp.ones((16, pixels), jnp.bfloat16)
    for slot in range(per_view):
        row_sum = jnp.dot(ones, gram_ref[slot], preferred_element_type=jnp.float32)
        defect[slot] = cover_ref[slot : slot + 1] - row_sum[:8]
    zrow = lax.broadcasted_iota(jnp.int32, (ext, RY), 0) + (me * rows - RIM)
    column = lax.broadcasted_iota(jnp.int32, (ext, RY), 1)

    pl.semaphore_wait(barrier, slabs - 1)

    def tv_step(step, scale):
        zmask = ((zrow >= 0) & (zrow < depth_total - 1)).astype(jnp.float32)
        cmask = (column < RY - 1).astype(jnp.float32)
        total = jnp.zeros((8, RY), jnp.float32)
        before = None
        here = xs[:ext, :RY]
        for i in range(tiles):
            lanes = slice(i * RY, (i + 1) * RY)
            dz = (xs[1 : ext + 1, lanes] - here) * zmask
            dc = (pltpu.roll(here, RY - 1, 1) - here) * cmask
            square = dz * dz + dc * dc + SMOOTHING
            if i < tiles - 1:
                after = xs[:ext, (i + 1) * RY : (i + 2) * RY]
                di = after - here
                square = square + di * di
            inverse = lax.rsqrt(square)
            fz = dz * inverse
            fc = dc * inverse
            fluxz[8:, lanes] = fz
            g = (fluxz[7 : ext + 7, lanes] - fz) + (pltpu.roll(fc, 1, 1) - fc)
            if before is not None:
                g = g + before
            if i < tiles - 1:
                fi = di * inverse
                g = g - fi
                before = fi
                here = after
            grad[:, lanes] = g
            mine = g[RIM : RIM + rows]
            total = total + jnp.sum((mine * mine).reshape(rows // 8, 8, RY), axis=0)
        own[step] = total
        sends = []
        for d in range(1, slabs):
            copy = pltpu.make_async_remote_copy(
                src_ref=own.at[step],
                dst_ref=stat.at[step, me],
                send_sem=stat_send.at[step, d],
                recv_sem=stat_recv.at[step, d],
                device_id=slab_device(lax.rem(me + d, slabs), gz),
                device_id_type=MESH,
            )
            copy.start()
            sends.append(copy)
        for d in range(1, slabs):
            source = lax.rem(me + slabs - d, slabs)
            pltpu.make_async_remote_copy(
                src_ref=own.at[step],
                dst_ref=stat.at[step, source],
                send_sem=stat_send.at[step, d],
                recv_sem=stat_recv.at[step, d],
                device_id=slab_device(source, gz),
                device_id_type=MESH,
            ).wait_recv()
        for d in range(1, slabs):
            source = lax.rem(me + slabs - d, slabs)
            total = total + stat[step, source]
        for copy in sends:
            copy.wait_send()
        mean = jnp.sum(total, keepdims=True) / (depth_total * pixels)
        factor = scale * lax.rsqrt(mean + NORM_GUARD)
        xs[:ext] = xs[:ext] - factor * grad[...]

    def sart(frame, n):
        x = xs[:ext]
        xb = x.astype(jnp.bfloat16)
        centre = jnp.sum(x, axis=1, keepdims=True) * (1.0 / pixels)
        width = 256
        for lo in range(0, pixels, width):
            lanes = slice(lo, lo + width)
            y = jnp.dot(xb, gram_ref[n, :, lanes], preferred_element_type=jnp.float32)
            y = y + centre * defect[n, 0:1, lanes]
            change = (back_ref[frame, n, :, lanes] - y) * (RELAXATION / cover_ref[n : n + 1, lanes])
            xs[:ext, lanes] = jnp.maximum(x[:, lanes] + change, 0.0)

    up, down = lax.rem(me + 1, slabs), lax.rem(me + slabs - 1, slabs)

    for frame in range(FRAMES):
        if frame > 0:
            copies = []
            for side, (source, target) in enumerate(((rows, up), (RIM, down))):
                copy = pltpu.make_async_remote_copy(
                    src_ref=xs.at[pl.ds(source, RIM)],
                    dst_ref=rim.at[frame - 1, side],
                    send_sem=rim_send.at[frame - 1, side],
                    recv_sem=rim_recv.at[frame - 1, side],
                    device_id=slab_device(target, gz),
                    device_id_type=MESH,
                )
                copy.start()
                copies.append(copy)
            for copy in copies:
                copy.wait()
            xs[:RIM] = rim[frame - 1, 0]
            xs[RIM + rows : ext] = rim[frame - 1, 1]

        def sweep_body(sweep, carry, frame=frame):
            for k in range(TV_STEPS):
                scale = jnp.float32(0.0)
                for s in range(SWEEPS):
                    value = STEP_SCALE * STEP_DECAY ** (s * TV_STEPS + k)
                    scale = jnp.where(sweep == s, jnp.float32(value), scale)
                tv_step((frame * SWEEPS + sweep) * TV_STEPS + k, scale)
            for n in range(per_view):
                sart(frame, n)
            return carry

        lax.fori_loop(0, SWEEPS, sweep_body, 0)
        out_ref[frame] = xs[RIM : RIM + rows]


def iterate(gram, back, cover, warm, slabs, gz):
    ext, pixels = warm.shape
    rows = ext - 2 * RIM
    steps = FRAMES * SWEEPS * TV_STEPS
    vmem = pl.BlockSpec(memory_space=pltpu.VMEM)
    return pl.pallas_call(
        functools.partial(iterate_kernel, slabs, gz),
        out_shape=jax.ShapeDtypeStruct((FRAMES, rows, pixels), jnp.float32),
        in_specs=[vmem] * 4,
        out_specs=vmem,
        scratch_shapes=[
            pltpu.VMEM((ext + 8, pixels), jnp.float32),
            pltpu.VMEM((ext, pixels), jnp.float32),
            pltpu.VMEM((ext + 8, pixels), jnp.float32),
            pltpu.VMEM((gram.shape[0], 8, pixels), jnp.float32),
            pltpu.VMEM((steps, 8, RY), jnp.float32),
            pltpu.VMEM((steps, slabs, 8, RY), jnp.float32),
            pltpu.VMEM((FRAMES - 1, 2, RIM, pixels), jnp.float32),
            pltpu.SemaphoreType.DMA((steps, slabs)),
            pltpu.SemaphoreType.DMA((steps, slabs)),
            pltpu.SemaphoreType.DMA((FRAMES - 1, 2)),
            pltpu.SemaphoreType.DMA((FRAMES - 1, 2)),
        ],
        compiler_params=pltpu.CompilerParams(
            collective_id=0, has_side_effects=True, vmem_limit_bytes=40 * 2**20
        ),
    )(gram, back, cover, warm)


def with_rims(block, dim, count):
    forward = [(i, (i + 1) % count) for i in range(count)]
    backward = [(target, source) for source, target in forward]
    axes = ("tm", "gz")
    low = lax.ppermute(
        lax.slice_in_dim(block, block.shape[dim] - RIM, None, axis=dim), axes, forward
    )
    high = lax.ppermute(lax.slice_in_dim(block, 0, RIM, axis=dim), axes, backward)
    return jnp.concatenate([low, block, high], axis=dim)


def body(tm, gz, sinogram, projector, warm_volume, view_order):
    slices, pixels = warm_volume.shape
    per_view = projector.shape[0]
    slabs = tm * gz
    slab = lax.axis_index("tm") * gz + lax.axis_index("gz")
    share = pixels // slabs
    ray_sums = jnp.sum(projector, axis=1, dtype=jnp.float32)
    cover = lax.psum(jnp.sum(projector, axis=2, dtype=jnp.float32), "view")
    rays = 1.0 / ray_sums[:, None, :]
    part = lax.dynamic_slice_in_dim(projector, slab * share, share, axis=1)
    weighted = (part.astype(jnp.float32) * rays).astype(jnp.bfloat16)
    measured = (sinogram.astype(jnp.float32) * rays[None]).astype(jnp.bfloat16)
    measured = jnp.swapaxes(measured, 0, 1).reshape(per_view, FRAMES * slices, -1)
    left = jnp.concatenate([weighted, measured], axis=1)
    product = jnp.einsum("jmd,jpd->jmp", left, projector, preferred_element_type=jnp.float32)
    gram = lax.psum_scatter(product[:, :share], "view", scatter_dimension=1, tiled=True)
    gram = lax.all_gather(
        gram.astype(jnp.bfloat16), ("tm", "gz", "view"), axis=1, tiled=True
    )
    back = lax.psum(product[:, share:], "view").reshape(per_view, FRAMES, slices, pixels)
    back = jnp.swapaxes(back, 0, 1)
    gram = jnp.take(gram, view_order, axis=0)
    back = jnp.take(back, view_order, axis=1)
    cover = jnp.take(cover, view_order, axis=0)
    return iterate(
        gram, with_rims(back, 2, slabs), cover, with_rims(warm_volume, 0, slabs), slabs, gz
    )


def solution(mesh):
    return jax.shard_map(
        functools.partial(body, mesh.shape["tm"], mesh.shape["gz"]),
        mesh=mesh,
        in_specs=(
            P(None, "view", ("tm", "gz"), None),
            P("view", None, None),
            P(("tm", "gz"), None),
            P(),
        ),
        out_specs=P(None, ("tm", "gz"), None),
        check_vma=False,
    )
```

```python
import functools

import jax
import jax.numpy as jnp
from jax import lax
from jax.experimental import pallas as pl
from jax.experimental.pallas import tpu as pltpu
from jax.sharding import PartitionSpec as P

RY = 128
FRAMES = 2
SWEEPS = 3
TV_STEPS = 2
RELAXATION = 0.9
STEP_SCALE = 0.3
STEP_DECAY = 0.7
SMOOTHING = 0.01
NORM_GUARD = 1e-06
RIM = 8

MESH = pl.DeviceIdType.MESH


def slab_device(index, gz):
    return {"tm": lax.div(index, gz), "gz": lax.rem(index, gz)}


def wrap(index, count):
    return lax.rem(index + count, count)


def remote(src, dst, send, recv, device):
    return pltpu.make_async_remote_copy(
        src_ref=src, dst_ref=dst, send_sem=send, recv_sem=recv,
        device_id=device, device_id_type=MESH,
    )


def iterate_kernel(
    slabs, gz, views, gram_part, back_part, cover_part, warm_ref, out_ref,
    gram, gram_in, back, back_in, cover_in, cover, xs, grad, fluxz, defect, own, stat, rim,
    cover_send, cover_recv, sum_send, sum_recv, view_send, view_recv, layer_send, layer_recv,
    pair_send, pair_recv, part_send, part_recv, full_send, full_recv, edge_send, edge_recv,
    stat_send, stat_recv, rim_send, rim_recv,
):
    me = lax.axis_index("tm") * gz + lax.axis_index("gz")
    mine = lax.axis_index("view")
    rows, pixels = warm_ref.shape
    ext = rows + 2 * RIM
    depth_total = slabs * rows
    per_view = gram.shape[0] // pixels
    tiles = pixels // RY
    share = pixels // slabs
    piece = per_view * share // views
    per_slot = views // per_view
    band = rows // views
    half = slabs // 2
    pair = lax.div(me, 2)
    side = lax.rem(me, 2)
    sibling = me + 1 - 2 * side
    up, down = wrap(me + 1, slabs), wrap(me - 1, slabs)

    def gram_rows(slab, view):
        start = lax.div(view, per_slot) * pixels + slab * share + lax.rem(view, per_slot) * piece
        return pl.ds(pl.multiple_of(start, 16), piece)

    def part_rows(view):
        return pl.ds(pl.multiple_of(view * piece, 16), piece)

    def band_rows(view, base):
        return pl.ds(pl.multiple_of(view * band + base, 8), band)

    def rim_copies(at):
        return [
            remote(
                xs.at[pl.ds(source, RIM)], rim.at[at, s],
                rim_send.at[at, s], rim_recv.at[at, s], slab_device(target, gz),
            )
            for s, (source, target) in enumerate(((rows, up), (RIM, down)))
        ]

    def take_rims(at):
        for copy in rim_copies(at):
            copy.wait()
        xs[:RIM] = rim[at, 0]
        xs[RIM + rows : ext] = rim[at, 1]

    def cover_copy(d, to):
        return remote(
            cover_part, cover_in.at[d], cover_send.at[d], cover_recv.at[d],
            {"view": wrap(mine + to, views)},
        )

    def sum_copy(d):
        target = wrap(mine + d, views)
        return remote(
            gram_part.at[part_rows(target)], gram_in.at[d],
            sum_send.at[d], sum_recv.at[d], {"view": target},
        )

    def view_copy(d, view, target):
        at = gram_rows(me, view)
        return remote(
            gram.at[at], gram.at[at], view_send.at[d], view_recv.at[d], {"view": target}
        )

    def layer_copy(d, e, slab, target):
        at = gram_rows(slab, wrap(mine - d, views))
        return remote(
            gram.at[at], gram.at[at], layer_send.at[d, e], layer_recv.at[d, e],
            slab_device(target, gz),
        )

    def mate(e):
        return wrap(pair + e, half) * 2 + side

    def pair_copy(d, e, slab):
        at = gram_rows(slab, wrap(mine - d, views))
        return remote(
            gram.at[at], gram.at[at], pair_send.at[d, e], pair_recv.at[d, e],
            slab_device(sibling, gz),
        )

    def part_copy(t, d):
        target = wrap(mine + d, views)
        return remote(
            back_part.at[t, :, band_rows(target, 0)], back_in.at[t, d],
            part_send.at[t, d], part_recv.at[t, d], {"view": target},
        )

    def full_copy(t, d, view, target):
        at = back.at[t, :, band_rows(view, RIM)]
        return remote(at, at, full_send.at[t, d], full_recv.at[t, d], {"view": target})

    def edge_copies(t):
        return [
            remote(
                back.at[t, :, pl.ds(source, RIM)], back.at[t, :, pl.ds(dest, RIM)],
                edge_send.at[t, s], edge_recv.at[t, s], slab_device(target, gz),
            )
            for s, (source, dest, target) in enumerate(
                ((rows, 0, up), (RIM, rows + RIM, down))
            )
        ]

    def sum_back(t):
        total = back_part[t, :, band_rows(mine, 0)]
        for d in range(1, views):
            part_copy(t, d).wait_recv()
            total = total + back_in[t, d]
        back[t, :, band_rows(mine, RIM)] = total
        for d in range(1, views):
            full_copy(t, d, mine, wrap(mine + d, views)).start()

    def spread_edges(t):
        for d in range(1, views):
            full_copy(t, d, wrap(mine - d, views), wrap(mine - d, views)).wait_recv()
        for copy in edge_copies(t):
            copy.start()

    def sum_gram():
        total = gram_part[part_rows(mine)].astype(jnp.float32)
        for d in range(1, views):
            sum_copy(d).wait_recv()
            total = total + gram_in[d].astype(jnp.float32)
        gram[gram_rows(me, mine)] = total.astype(jnp.bfloat16)
        for d in range(1, views):
            view_copy(d, mine, wrap(mine + d, views)).start()
        for e in range(1, half):
            layer_copy(0, e, me, mate(e)).start()
        pair_copy(0, 0, me).start()

    def gather_gram():
        for d in range(1, views):
            view_copy(d, wrap(mine - d, views), wrap(mine - d, views)).wait_recv()
            for e in range(1, half):
                layer_copy(d, e, me, mate(e)).start()
            pair_copy(d, 0, me).start()
        for d in range(views):
            for e in range(1, half):
                layer_copy(d, e, mate(-e), mate(-e)).wait_recv()
                pair_copy(d, e, mate(-e)).start()
        for d in range(views):
            for e in range(half):
                pair_copy(d, e, mate(-e) + 1 - 2 * side).wait_recv()

    def weigh():
        for d in range(1, views):
            cover_copy(d, d).wait_recv()
        total = cover_part[...]
        for d in range(1, views):
            total = total + cover_in[d]
        cover[...] = RELAXATION / total
        ones = jnp.ones((16, pixels), jnp.bfloat16)
        for slot in range(per_view):
            row_sum = jnp.dot(
                ones, gram[slot * pixels : (slot + 1) * pixels],
                preferred_element_type=jnp.float32,
            )
            defect[slot] = total[slot : slot + 1] - row_sum[:8]

    barrier = pltpu.get_barrier_semaphore()
    for d in range(1, slabs):
        pl.semaphore_signal(
            barrier, inc=1, device_id=slab_device(wrap(me + d, slabs), gz), device_id_type=MESH
        )
    for d in range(1, views):
        pl.semaphore_signal(
            barrier, inc=1, device_id={"view": wrap(mine + d, views)}, device_id_type=MESH
        )

    xs[RIM : RIM + rows] = warm_ref[...]
    xs[ext:] = jnp.zeros((8, pixels), jnp.float32)
    fluxz[:8] = jnp.zeros((8, pixels), jnp.float32)
    zrow = lax.broadcasted_iota(jnp.int32, (ext, RY), 0) + (me * rows - RIM)
    column = lax.broadcasted_iota(jnp.int32, (ext, RY), 1)

    pl.semaphore_wait(barrier, slabs + views - 2)
    for copy in rim_copies(0):
        copy.start()
    for d in range(1, views):
        sum_copy(d).start()
    for d in range(1, views):
        cover_copy(d, d).start()
    for d in range(1, views):
        part_copy(0, d).start()
    take_rims(0)

    def tv_step(step, scale):
        zmask = ((zrow >= 0) & (zrow < depth_total - 1)).astype(jnp.float32)
        cmask = (column < RY - 1).astype(jnp.float32)
        total = jnp.zeros((8, RY), jnp.float32)
        before = None
        here = xs[:ext, :RY]
        for i in range(tiles):
            lanes = slice(i * RY, (i + 1) * RY)
            dz = (xs[1 : ext + 1, lanes] - here) * zmask
            dc = (pltpu.roll(here, RY - 1, 1) - here) * cmask
            square = dz * dz + dc * dc + SMOOTHING
            if i < tiles - 1:
                after = xs[:ext, (i + 1) * RY : (i + 2) * RY]
                di = after - here
                square = square + di * di
            inverse = lax.rsqrt(square)
            fz = dz * inverse
            fc = dc * inverse
            fluxz[8:, lanes] = fz
            g = (fluxz[7 : ext + 7, lanes] - fz) + (pltpu.roll(fc, 1, 1) - fc)
            if before is not None:
                g = g + before
            if i < tiles - 1:
                fi = di * inverse
                g = g - fi
                before = fi
                here = after
            grad[:, lanes] = g
            inner = g[RIM : RIM + rows]
            total = total + jnp.sum((inner * inner).reshape(rows // 8, 8, RY), axis=0)
        own[step] = total
        sends = []
        for d in range(1, slabs):
            copy = pltpu.make_async_remote_copy(
                src_ref=own.at[step],
                dst_ref=stat.at[step, me],
                send_sem=stat_send.at[step, d],
                recv_sem=stat_recv.at[step, d],
                device_id=slab_device(lax.rem(me + d, slabs), gz),
                device_id_type=MESH,
            )
            copy.start()
            sends.append(copy)
        for d in range(1, slabs):
            source = lax.rem(me + slabs - d, slabs)
            pltpu.make_async_remote_copy(
                src_ref=own.at[step],
                dst_ref=stat.at[step, source],
                send_sem=stat_send.at[step, d],
                recv_sem=stat_recv.at[step, d],
                device_id=slab_device(source, gz),
                device_id_type=MESH,
            ).wait_recv()
        for d in range(1, slabs):
            source = lax.rem(me + slabs - d, slabs)
            total = total + stat[step, source]
        for copy in sends:
            copy.wait_send()
        mean = jnp.sum(total, keepdims=True) / (depth_total * pixels)
        factor = scale * lax.rsqrt(mean + NORM_GUARD)
        xs[:ext] = xs[:ext] - factor * grad[...]

    def sart(frame, n):
        x = xs[:ext]
        xb = x.astype(jnp.bfloat16)
        centre = jnp.sum(x, axis=1, keepdims=True) * (1.0 / pixels)
        width = 256
        for lo in range(0, pixels, width):
            lanes = slice(lo, lo + width)
            y = jnp.dot(
                xb, gram[n * pixels : (n + 1) * pixels, lanes], preferred_element_type=jnp.float32
            )
            y = y + centre * defect[n, 0:1, lanes]
            change = (back[frame, n, :, lanes] - y) * cover[n : n + 1, lanes]
            xs[:ext, lanes] = jnp.maximum(x[:, lanes] + change, 0.0)

    def sweep_body(sweep, carry):
        frame = lax.div(sweep, SWEEPS)
        for at in range(1, FRAMES):
            @pl.when(sweep == at * SWEEPS)
            def _():
                for copy in rim_copies(at):
                    copy.start()
                take_rims(at)
                for copy in edge_copies(at):
                    copy.wait_recv()

        for k in range(TV_STEPS):
            scale = jnp.float32(0.0)
            for s in range(SWEEPS):
                value = STEP_SCALE * STEP_DECAY ** (s * TV_STEPS + k)
                scale = jnp.where(lax.rem(sweep, SWEEPS) == s, jnp.float32(value), scale)
            tv_step(sweep * TV_STEPS + k, scale)
            if k == 0:
                @pl.when(sweep == 0)
                def _():
                    sum_gram()
                    sum_back(0)

        @pl.when(sweep == 0)
        def _():
            gather_gram()
            spread_edges(0)
            for t in range(1, FRAMES):
                for d in range(1, views):
                    part_copy(t, d).start()
            weigh()
            for copy in edge_copies(0):
                copy.wait_recv()

        for t in range(1, FRAMES):
            @pl.when(sweep == t * SWEEPS - 2)
            def _():
                sum_back(t)

            @pl.when(sweep == t * SWEEPS - 1)
            def _():
                spread_edges(t)

        for n in range(per_view):
            sart(frame, n)

        for t in range(FRAMES):
            @pl.when(sweep == (t + 1) * SWEEPS - 1)
            def _():
                out_ref[t] = xs[RIM : RIM + rows]
        return carry

    lax.fori_loop(0, FRAMES * SWEEPS, sweep_body, 0)

    for d in range(1, views):
        target = wrap(mine + d, views)
        cover_copy(d, d).wait_send()
        sum_copy(d).wait_send()
        view_copy(d, mine, target).wait_send()
        for t in range(FRAMES):
            part_copy(t, d).wait_send()
            full_copy(t, d, mine, target).wait_send()
    for d in range(views):
        for e in range(half):
            if e > 0:
                layer_copy(d, e, me, mate(e)).wait_send()
            pair_copy(d, e, mate(-e)).wait_send()
    for t in range(FRAMES):
        for copy in edge_copies(t):
            copy.wait_send()


def iterate(gram_part, back_part, cover_part, warm, slabs, gz, views):
    rows, pixels = warm.shape
    ext = rows + 2 * RIM
    steps = FRAMES * SWEEPS * TV_STEPS
    per_view = back_part.shape[1]
    piece = gram_part.shape[0] // views
    band = rows // views
    vmem = pl.BlockSpec(memory_space=pltpu.VMEM)
    dma = pltpu.SemaphoreType.DMA
    f32 = jnp.float32
    return pl.pallas_call(
        functools.partial(iterate_kernel, slabs, gz, views),
        out_shape=jax.ShapeDtypeStruct((FRAMES, rows, pixels), f32),
        in_specs=[vmem] * 4,
        out_specs=vmem,
        scratch_shapes=[
            pltpu.VMEM((per_view * pixels, pixels), jnp.bfloat16),
            pltpu.VMEM((views, piece, pixels), jnp.bfloat16),
            pltpu.VMEM((FRAMES, per_view, ext, pixels), f32),
            pltpu.VMEM((FRAMES, views, per_view, band, pixels), f32),
            pltpu.VMEM((views, 8, pixels), f32),
            pltpu.VMEM((8, pixels), f32),
            pltpu.VMEM((ext + 8, pixels), f32),
            pltpu.VMEM((ext, pixels), f32),
            pltpu.VMEM((ext + 8, pixels), f32),
            pltpu.VMEM((per_view, 8, pixels), f32),
            pltpu.VMEM((steps, 8, RY), f32),
            pltpu.VMEM((steps, slabs, 8, RY), f32),
            pltpu.VMEM((FRAMES, 2, RIM, pixels), f32),
            dma((views,)), dma((views,)), dma((views,)), dma((views,)), dma((views,)), dma((views,)),
            dma((views, slabs // 2)), dma((views, slabs // 2)),
            dma((views, slabs // 2)), dma((views, slabs // 2)),
            dma((FRAMES, views)), dma((FRAMES, views)), dma((FRAMES, views)), dma((FRAMES, views)),
            dma((FRAMES, 2)), dma((FRAMES, 2)),
            dma((steps, slabs)), dma((steps, slabs)),
            dma((FRAMES, 2)), dma((FRAMES, 2)),
        ],
        compiler_params=pltpu.CompilerParams(
            collective_id=0, has_side_effects=True, vmem_limit_bytes=40 * 2**20
        ),
    )(gram_part, back_part, cover_part, warm)


def body(tm, gz, views, sinogram, projector, warm_volume, view_order):
    slices, pixels = warm_volume.shape
    per_view = projector.shape[0]
    slabs = tm * gz
    slab = lax.axis_index("tm") * gz + lax.axis_index("gz")
    share = pixels // slabs
    ray_sums = jnp.sum(projector, axis=1, dtype=jnp.float32)
    cover = jnp.sum(projector, axis=2, dtype=jnp.float32)
    rays = 1.0 / ray_sums[:, None, :]
    part = lax.dynamic_slice_in_dim(projector, slab * share, share, axis=1)
    weighted = (part.astype(jnp.float32) * rays).astype(jnp.bfloat16)
    measured = (sinogram.astype(jnp.float32) * rays[None]).astype(jnp.bfloat16)
    measured = jnp.swapaxes(measured, 0, 1).reshape(per_view, FRAMES * slices, -1)
    left = jnp.concatenate([weighted, measured], axis=1)
    product = jnp.einsum("jmd,jpd->jmp", left, projector, preferred_element_type=jnp.float32)

    def ordered(block):
        return jnp.concatenate(
            [lax.dynamic_slice_in_dim(block, view_order[n], 1, axis=0) for n in range(per_view)],
            axis=0,
        )

    product = ordered(product)
    gram = product[:, :share].astype(jnp.bfloat16).reshape(per_view * share, pixels)
    back = jnp.swapaxes(product[:, share:].reshape(per_view, FRAMES, slices, pixels), 0, 1)
    cover = jnp.pad(ordered(cover), ((0, 8 - per_view), (0, 0)), constant_values=1.0)
    return iterate(gram, back, cover, warm_volume, slabs, gz, views)


def solution(mesh):
    return jax.shard_map(
        functools.partial(body, mesh.shape["tm"], mesh.shape["gz"], mesh.shape["view"]),
        mesh=mesh,
        in_specs=(
            P(None, "view", ("tm", "gz"), None),
            P("view", None, None),
            P(("tm", "gz"), None),
            P(),
        ),
        out_specs=P(None, ("tm", "gz"), None),
        check_vma=False,
    )
```

```python
import functools

import jax
import jax.numpy as jnp
from jax import lax
from jax.experimental import pallas as pl
from jax.experimental.pallas import tpu as pltpu
from jax.sharding import PartitionSpec as P

RY = 128
FRAMES = 2
SWEEPS = 3
TV_STEPS = 2
RELAXATION = 0.9
STEP_SCALE = 0.3
STEP_DECAY = 0.7
SMOOTHING = 0.01
NORM_GUARD = 1e-06
RIM = 8

MESH = pl.DeviceIdType.MESH


def slab_device(index, gz):
    return {"tm": lax.div(index, gz), "gz": lax.rem(index, gz)}


def wrap(index, count):
    return lax.rem(index + count, count)


def remote(src, dst, send, recv, device):
    return pltpu.make_async_remote_copy(
        src_ref=src, dst_ref=dst, send_sem=send, recv_sem=recv,
        device_id=device, device_id_type=MESH,
    )


def iterate_kernel(
    slabs, gz, views, gram_part, back_part, cover_part, warm_ref, out_ref,
    gram, gram_in, back, back_in, cover_in, cover, xs, grad, fluxz, defect, own, stat, rim,
    cover_send, cover_recv, sum_send, sum_recv, view_send, view_recv, layer_send, layer_recv,
    pair_send, pair_recv, part_send, part_recv, full_send, full_recv, edge_send, edge_recv,
    stat_send, stat_recv, rim_send, rim_recv,
):
    me = lax.axis_index("tm") * gz + lax.axis_index("gz")
    mine = lax.axis_index("view")
    rows, pixels = warm_ref.shape
    ext = rows + 2 * RIM
    depth_total = slabs * rows
    per_view = gram.shape[0] // pixels
    tiles = pixels // RY
    share = pixels // slabs
    piece = per_view * share // views
    per_slot = views // per_view
    band = rows // views
    half = slabs // 2
    pair = lax.div(me, 2)
    side = lax.rem(me, 2)
    sibling = me + 1 - 2 * side
    up, down = wrap(me + 1, slabs), wrap(me - 1, slabs)

    def gram_rows(slab, view):
        start = lax.div(view, per_slot) * pixels + slab * share + lax.rem(view, per_slot) * piece
        return pl.ds(pl.multiple_of(start, 16), piece)

    def part_rows(view):
        return pl.ds(pl.multiple_of(view * piece, 16), piece)

    def band_rows(view, base):
        return pl.ds(pl.multiple_of(view * band + base, 8), band)

    def rim_copies(at):
        return [
            remote(
                xs.at[pl.ds(source, RIM)], rim.at[at, s],
                rim_send.at[at, s], rim_recv.at[at, s], slab_device(target, gz),
            )
            for s, (source, target) in enumerate(((rows, up), (RIM, down)))
        ]

    def take_rims(at):
        for copy in rim_copies(at):
            copy.wait()
        xs[:RIM] = rim[at, 0]
        xs[RIM + rows : ext] = rim[at, 1]

    def cover_copy(d, to):
        return remote(
            cover_part, cover_in.at[d], cover_send.at[d], cover_recv.at[d],
            {"view": wrap(mine + to, views)},
        )

    def sum_copy(d):
        target = wrap(mine + d, views)
        return remote(
            gram_part.at[part_rows(target)], gram_in.at[d],
            sum_send.at[d], sum_recv.at[d], {"view": target},
        )

    def view_copy(d, view, target):
        at = gram_rows(me, view)
        return remote(
            gram.at[at], gram.at[at], view_send.at[d], view_recv.at[d], {"view": target}
        )

    def layer_copy(d, e, slab, target):
        at = gram_rows(slab, wrap(mine - d, views))
        return remote(
            gram.at[at], gram.at[at], layer_send.at[d, e], layer_recv.at[d, e],
            slab_device(target, gz),
        )

    def mate(e):
        return wrap(pair + e, half) * 2 + side

    def pair_copy(d, e, slab):
        at = gram_rows(slab, wrap(mine - d, views))
        return remote(
            gram.at[at], gram.at[at], pair_send.at[d, e], pair_recv.at[d, e],
            slab_device(sibling, gz),
        )

    def part_copy(t, d):
        target = wrap(mine + d, views)
        return remote(
            back_part.at[t, :, band_rows(target, 0)], back_in.at[t, d],
            part_send.at[t, d], part_recv.at[t, d], {"view": target},
        )

    def full_copy(t, d, view, target):
        at = back.at[t, :, band_rows(view, RIM)]
        return remote(at, at, full_send.at[t, d], full_recv.at[t, d], {"view": target})

    def edge_copies(t):
        return [
            remote(
                back.at[t, :, pl.ds(source, RIM)], back.at[t, :, pl.ds(dest, RIM)],
                edge_send.at[t, s], edge_recv.at[t, s], slab_device(target, gz),
            )
            for s, (source, dest, target) in enumerate(
                ((rows, 0, up), (RIM, rows + RIM, down))
            )
        ]

    def sum_back(t):
        total = back_part[t, :, band_rows(mine, 0)]
        for d in range(1, views):
            part_copy(t, d).wait_recv()
            total = total + back_in[t, d]
        back[t, :, band_rows(mine, RIM)] = total
        for d in range(1, views):
            full_copy(t, d, mine, wrap(mine + d, views)).start()

    def spread_edges(t):
        for d in range(1, views):
            full_copy(t, d, wrap(mine - d, views), wrap(mine - d, views)).wait_recv()
        for copy in edge_copies(t):
            copy.start()

    def sum_gram():
        total = gram_part[part_rows(mine)].astype(jnp.float32)
        for d in range(1, views):
            sum_copy(d).wait_recv()
            total = total + gram_in[d].astype(jnp.float32)
        gram[gram_rows(me, mine)] = total.astype(jnp.bfloat16)
        for d in range(1, views):
            view_copy(d, mine, wrap(mine + d, views)).start()
        for e in range(1, half):
            layer_copy(0, e, me, mate(e)).start()
        pair_copy(0, 0, me).start()
        for d in range(1, views):
            part_copy(0, d).start()

    def gather_gram():
        for d in range(1, views):
            view_copy(d, wrap(mine - d, views), wrap(mine - d, views)).wait_recv()
            for e in range(1, half):
                layer_copy(d, e, me, mate(e)).start()
            pair_copy(d, 0, me).start()
        sum_back(0)
        for d in range(views):
            for e in range(1, half):
                layer_copy(d, e, mate(-e), mate(-e)).wait_recv()
                pair_copy(d, e, mate(-e)).start()
        for d in range(views):
            for e in range(half):
                pair_copy(d, e, mate(-e) + 1 - 2 * side).wait_recv()

    def weigh():
        for d in range(1, views):
            cover_copy(d, d).wait_recv()
        total = cover_part[...]
        for d in range(1, views):
            total = total + cover_in[d]
        cover[...] = RELAXATION / total
        ones = jnp.ones((16, pixels), jnp.bfloat16)
        for slot in range(per_view):
            row_sum = jnp.dot(
                ones, gram[slot * pixels : (slot + 1) * pixels],
                preferred_element_type=jnp.float32,
            )
            defect[slot] = total[slot : slot + 1] - row_sum[:8]

    barrier = pltpu.get_barrier_semaphore()
    for d in range(1, slabs):
        pl.semaphore_signal(
            barrier, inc=1, device_id=slab_device(wrap(me + d, slabs), gz), device_id_type=MESH
        )
    for d in range(1, views):
        pl.semaphore_signal(
            barrier, inc=1, device_id={"view": wrap(mine + d, views)}, device_id_type=MESH
        )

    xs[RIM : RIM + rows] = warm_ref[...]
    xs[ext:] = jnp.zeros((8, pixels), jnp.float32)
    fluxz[:8] = jnp.zeros((8, pixels), jnp.float32)
    zrow = lax.broadcasted_iota(jnp.int32, (ext, RY), 0) + (me * rows - RIM)
    column = lax.broadcasted_iota(jnp.int32, (ext, RY), 1)

    pl.semaphore_wait(barrier, slabs + views - 2)
    for copy in rim_copies(0):
        copy.start()
    for d in range(1, views):
        sum_copy(d).start()
    for d in range(1, views):
        cover_copy(d, d).start()
    take_rims(0)

    def tv_step(step, scale):
        zmask = ((zrow >= 0) & (zrow < depth_total - 1)).astype(jnp.float32)
        cmask = (column < RY - 1).astype(jnp.float32)
        total = jnp.zeros((8, RY), jnp.float32)
        before = None
        here = xs[:ext, :RY]
        for i in range(tiles):
            lanes = slice(i * RY, (i + 1) * RY)
            dz = (xs[1 : ext + 1, lanes] - here) * zmask
            dc = (pltpu.roll(here, RY - 1, 1) - here) * cmask
            square = dz * dz + dc * dc + SMOOTHING
            if i < tiles - 1:
                after = xs[:ext, (i + 1) * RY : (i + 2) * RY]
                di = after - here
                square = square + di * di
            inverse = lax.rsqrt(square)
            fz = dz * inverse
            fc = dc * inverse
            fluxz[8:, lanes] = fz
            g = (fluxz[7 : ext + 7, lanes] - fz) + (pltpu.roll(fc, 1, 1) - fc)
            if before is not None:
                g = g + before
            if i < tiles - 1:
                fi = di * inverse
                g = g - fi
                before = fi
                here = after
            grad[:, lanes] = g
            inner = g[RIM : RIM + rows]
            total = total + jnp.sum((inner * inner).reshape(rows // 8, 8, RY), axis=0)
        own[step] = total
        sends = []
        for d in range(1, slabs):
            copy = pltpu.make_async_remote_copy(
                src_ref=own.at[step],
                dst_ref=stat.at[step, me],
                send_sem=stat_send.at[step, d],
                recv_sem=stat_recv.at[step, d],
                device_id=slab_device(lax.rem(me + d, slabs), gz),
                device_id_type=MESH,
            )
            copy.start()
            sends.append(copy)
        for d in range(1, slabs):
            source = lax.rem(me + slabs - d, slabs)
            pltpu.make_async_remote_copy(
                src_ref=own.at[step],
                dst_ref=stat.at[step, source],
                send_sem=stat_send.at[step, d],
                recv_sem=stat_recv.at[step, d],
                device_id=slab_device(source, gz),
                device_id_type=MESH,
            ).wait_recv()
        for d in range(1, slabs):
            source = lax.rem(me + slabs - d, slabs)
            total = total + stat[step, source]
        for copy in sends:
            copy.wait_send()
        mean = jnp.sum(total, keepdims=True) / (depth_total * pixels)
        factor = scale * lax.rsqrt(mean + NORM_GUARD)
        xs[:ext] = xs[:ext] - factor * grad[...]

    def sart(frame, n):
        x = xs[:ext]
        xb = x.astype(jnp.bfloat16)
        centre = jnp.sum(x, axis=1, keepdims=True) * (1.0 / pixels)
        width = 256
        for lo in range(0, pixels, width):
            lanes = slice(lo, lo + width)
            y = jnp.dot(
                xb, gram[n * pixels : (n + 1) * pixels, lanes], preferred_element_type=jnp.float32
            )
            y = y + centre * defect[n, 0:1, lanes]
            change = (back[frame, n, :, lanes] - y) * cover[n : n + 1, lanes]
            xs[:ext, lanes] = jnp.maximum(x[:, lanes] + change, 0.0)

    def sweep_body(sweep, carry):
        frame = lax.div(sweep, SWEEPS)
        for at in range(1, FRAMES):
            @pl.when(sweep == at * SWEEPS)
            def _():
                for copy in rim_copies(at):
                    copy.start()
                take_rims(at)
                for copy in edge_copies(at):
                    copy.wait_recv()

        for k in range(TV_STEPS):
            scale = jnp.float32(0.0)
            for s in range(SWEEPS):
                value = STEP_SCALE * STEP_DECAY ** (s * TV_STEPS + k)
                scale = jnp.where(lax.rem(sweep, SWEEPS) == s, jnp.float32(value), scale)
            tv_step(sweep * TV_STEPS + k, scale)
            if k == 0:
                @pl.when(sweep == 0)
                def _():
                    sum_gram()

        @pl.when(sweep == 0)
        def _():
            gather_gram()
            spread_edges(0)
            for t in range(1, FRAMES):
                for d in range(1, views):
                    part_copy(t, d).start()
            weigh()
            for copy in edge_copies(0):
                copy.wait_recv()

        for t in range(1, FRAMES):
            @pl.when(sweep == t * SWEEPS - 2)
            def _():
                sum_back(t)

            @pl.when(sweep == t * SWEEPS - 1)
            def _():
                spread_edges(t)

        for n in range(per_view):
            sart(frame, n)

        for t in range(FRAMES):
            @pl.when(sweep == (t + 1) * SWEEPS - 1)
            def _():
                out_ref[t] = xs[RIM : RIM + rows]
        return carry

    lax.fori_loop(0, FRAMES * SWEEPS, sweep_body, 0)

    for d in range(1, views):
        target = wrap(mine + d, views)
        cover_copy(d, d).wait_send()
        sum_copy(d).wait_send()
        view_copy(d, mine, target).wait_send()
        for t in range(FRAMES):
            part_copy(t, d).wait_send()
            full_copy(t, d, mine, target).wait_send()
    for d in range(views):
        for e in range(half):
            if e > 0:
                layer_copy(d, e, me, mate(e)).wait_send()
            pair_copy(d, e, mate(-e)).wait_send()
    for t in range(FRAMES):
        for copy in edge_copies(t):
            copy.wait_send()


def iterate(gram_part, back_part, cover_part, warm, slabs, gz, views):
    rows, pixels = warm.shape
    ext = rows + 2 * RIM
    steps = FRAMES * SWEEPS * TV_STEPS
    per_view = back_part.shape[1]
    piece = gram_part.shape[0] // views
    band = rows // views
    vmem = pl.BlockSpec(memory_space=pltpu.VMEM)
    dma = pltpu.SemaphoreType.DMA
    f32 = jnp.float32
    return pl.pallas_call(
        functools.partial(iterate_kernel, slabs, gz, views),
        out_shape=jax.ShapeDtypeStruct((FRAMES, rows, pixels), f32),
        in_specs=[vmem] * 4,
        out_specs=vmem,
        scratch_shapes=[
            pltpu.VMEM((per_view * pixels, pixels), jnp.bfloat16),
            pltpu.VMEM((views, piece, pixels), jnp.bfloat16),
            pltpu.VMEM((FRAMES, per_view, ext, pixels), f32),
            pltpu.VMEM((FRAMES, views, per_view, band, pixels), f32),
            pltpu.VMEM((views, 8, pixels), f32),
            pltpu.VMEM((8, pixels), f32),
            pltpu.VMEM((ext + 8, pixels), f32),
            pltpu.VMEM((ext, pixels), f32),
            pltpu.VMEM((ext + 8, pixels), f32),
            pltpu.VMEM((per_view, 8, pixels), f32),
            pltpu.VMEM((steps, 8, RY), f32),
            pltpu.VMEM((steps, slabs, 8, RY), f32),
            pltpu.VMEM((FRAMES, 2, RIM, pixels), f32),
            dma((views,)), dma((views,)), dma((views,)), dma((views,)), dma((views,)), dma((views,)),
            dma((views, slabs // 2)), dma((views, slabs // 2)),
            dma((views, slabs // 2)), dma((views, slabs // 2)),
            dma((FRAMES, views)), dma((FRAMES, views)), dma((FRAMES, views)), dma((FRAMES, views)),
            dma((FRAMES, 2)), dma((FRAMES, 2)),
            dma((steps, slabs)), dma((steps, slabs)),
            dma((FRAMES, 2)), dma((FRAMES, 2)),
        ],
        compiler_params=pltpu.CompilerParams(
            collective_id=0, has_side_effects=True, vmem_limit_bytes=40 * 2**20
        ),
    )(gram_part, back_part, cover_part, warm)


def body(tm, gz, views, sinogram, projector, warm_volume, view_order):
    slices, pixels = warm_volume.shape
    per_view = projector.shape[0]
    slabs = tm * gz
    slab = lax.axis_index("tm") * gz + lax.axis_index("gz")
    share = pixels // slabs
    ray_sums = jnp.sum(projector, axis=1, dtype=jnp.float32)
    rays = 1.0 / ray_sums[:, None, :]
    part = lax.dynamic_slice_in_dim(projector, slab * share, share, axis=1)
    weighted = (part.astype(jnp.float32) * rays).astype(jnp.bfloat16)
    measured = (sinogram.astype(jnp.float32) * rays[None]).astype(jnp.bfloat16)
    measured = jnp.swapaxes(measured, 0, 1).reshape(per_view, FRAMES * slices, -1)
    left = jnp.concatenate(
        [weighted, measured, jnp.ones((per_view, 8, projector.shape[2]), jnp.bfloat16)], axis=1
    )
    product = jnp.einsum("jmd,jpd->jmp", left, projector, preferred_element_type=jnp.float32)

    def ordered(block):
        return jnp.concatenate(
            [lax.dynamic_slice_in_dim(block, view_order[n], 1, axis=0) for n in range(per_view)],
            axis=0,
        )

    product = ordered(product)
    filled = share + FRAMES * slices
    gram = product[:, :share].astype(jnp.bfloat16).reshape(per_view * share, pixels)
    back = jnp.swapaxes(product[:, share:filled].reshape(per_view, FRAMES, slices, pixels), 0, 1)
    cover = jnp.pad(product[:, filled], ((0, 8 - per_view), (0, 0)), constant_values=1.0)
    return iterate(gram, back, cover, warm_volume, slabs, gz, views)


def solution(mesh):
    return jax.shard_map(
        functools.partial(body, mesh.shape["tm"], mesh.shape["gz"], mesh.shape["view"]),
        mesh=mesh,
        in_specs=(
            P(None, "view", ("tm", "gz"), None),
            P("view", None, None),
            P(("tm", "gz"), None),
            P(),
        ),
        out_specs=P(None, ("tm", "gz"), None),
        check_vma=False,
    )
```

```python
import functools

import jax
import jax.numpy as jnp
from jax import lax
from jax.experimental import pallas as pl
from jax.experimental.pallas import tpu as pltpu
from jax.sharding import PartitionSpec as P

RY = 128
FRAMES = 2
SWEEPS = 3
TV_STEPS = 2
RELAXATION = 0.9
STEP_SCALE = 0.3
STEP_DECAY = 0.7
SMOOTHING = 0.01
NORM_GUARD = 1e-06
RIM = 8

MESH = pl.DeviceIdType.MESH


def slab_device(index, gz):
    return {"tm": lax.div(index, gz), "gz": lax.rem(index, gz)}


def wrap(index, count):
    return lax.rem(index + count, count)


def remote(src, dst, send, recv, device):
    return pltpu.make_async_remote_copy(
        src_ref=src, dst_ref=dst, send_sem=send, recv_sem=recv,
        device_id=device, device_id_type=MESH,
    )


def iterate_kernel(
    slabs, gz, views, gram_part, back_part, cover_part, warm_ref, out_ref,
    gram, gram_in, back, back_in, cover_in, cover, xs, grad, fluxz, defect, own, stat, rim,
    cover_send, cover_recv, sum_send, sum_recv, view_send, view_recv, layer_send, layer_recv,
    pair_send, pair_recv, part_send, part_recv, full_send, full_recv, edge_send, edge_recv,
    stat_send, stat_recv, rim_send, rim_recv,
):
    me = lax.axis_index("tm") * gz + lax.axis_index("gz")
    mine = lax.axis_index("view")
    rows, pixels = warm_ref.shape
    ext = rows + 2 * RIM
    depth_total = slabs * rows
    per_view = gram.shape[0] // pixels
    tiles = pixels // RY
    share = pixels // slabs
    piece = per_view * share // views
    per_slot = views // per_view
    band = rows // views
    half = slabs // 2
    pair = lax.div(me, 2)
    side = lax.rem(me, 2)
    sibling = me + 1 - 2 * side
    up, down = wrap(me + 1, slabs), wrap(me - 1, slabs)

    def gram_rows(slab, view):
        start = lax.div(view, per_slot) * pixels + slab * share + lax.rem(view, per_slot) * piece
        return pl.ds(pl.multiple_of(start, 16), piece)

    def part_rows(view):
        return pl.ds(pl.multiple_of(view * piece, 16), piece)

    def band_rows(view, base):
        return pl.ds(pl.multiple_of(view * band + base, 8), band)

    def rim_copies(at):
        return [
            remote(
                xs.at[pl.ds(source, RIM)], rim.at[at, s],
                rim_send.at[at, s], rim_recv.at[at, s], slab_device(target, gz),
            )
            for s, (source, target) in enumerate(((rows, up), (RIM, down)))
        ]

    def take_rims(at):
        for copy in rim_copies(at):
            copy.wait()
        xs[:RIM] = rim[at, 0]
        xs[RIM + rows : ext] = rim[at, 1]

    def cover_copy(d, to):
        return remote(
            cover_part, cover_in.at[d], cover_send.at[d], cover_recv.at[d],
            {"view": wrap(mine + to, views)},
        )

    def sum_copy(d):
        target = wrap(mine + d, views)
        return remote(
            gram_part.at[part_rows(target)], gram_in.at[d],
            sum_send.at[d], sum_recv.at[d], {"view": target},
        )

    def view_copy(d, view, target):
        at = gram_rows(me, view)
        return remote(
            gram.at[at], gram.at[at], view_send.at[d], view_recv.at[d], {"view": target}
        )

    def layer_copy(d, e, slab, target):
        at = gram_rows(slab, wrap(mine - d, views))
        return remote(
            gram.at[at], gram.at[at], layer_send.at[d, e], layer_recv.at[d, e],
            slab_device(target, gz),
        )

    def mate(e):
        return wrap(pair + e, half) * 2 + side

    def pair_copy(d, e, slab):
        at = gram_rows(slab, wrap(mine - d, views))
        return remote(
            gram.at[at], gram.at[at], pair_send.at[d, e], pair_recv.at[d, e],
            slab_device(sibling, gz),
        )

    def part_copy(t, d):
        target = wrap(mine + d, views)
        return remote(
            back_part.at[t, :, band_rows(target, 0)], back_in.at[t, d],
            part_send.at[t, d], part_recv.at[t, d], {"view": target},
        )

    def full_copy(t, d, view, target):
        at = back.at[t, :, band_rows(view, RIM)]
        return remote(at, at, full_send.at[t, d], full_recv.at[t, d], {"view": target})

    def edge_copies(t):
        return [
            remote(
                back.at[t, :, pl.ds(source, RIM)], back.at[t, :, pl.ds(dest, RIM)],
                edge_send.at[t, s], edge_recv.at[t, s], slab_device(target, gz),
            )
            for s, (source, dest, target) in enumerate(
                ((rows, 0, up), (RIM, rows + RIM, down))
            )
        ]

    def sum_back(t):
        total = back_part[t, :, band_rows(mine, 0)]
        for d in range(1, views):
            part_copy(t, d).wait_recv()
            total = total + back_in[t, d]
        back[t, :, band_rows(mine, RIM)] = total
        for d in range(1, views):
            full_copy(t, d, mine, wrap(mine + d, views)).start()

    def spread_edges(t):
        for d in range(1, views):
            full_copy(t, d, wrap(mine - d, views), wrap(mine - d, views)).wait_recv()
        for copy in edge_copies(t):
            copy.start()

    def sum_gram():
        total = gram_part[part_rows(mine)].astype(jnp.float32)
        for d in range(1, views):
            sum_copy(d).wait_recv()
            total = total + gram_in[d].astype(jnp.float32)
        gram[gram_rows(me, mine)] = total.astype(jnp.bfloat16)
        for d in range(1, views):
            view_copy(d, mine, wrap(mine + d, views)).start()
        for e in range(1, half):
            layer_copy(0, e, me, mate(e)).start()
        pair_copy(0, 0, me).start()
        for d in range(1, views):
            part_copy(0, d).start()

    def gather_gram():
        for d in range(1, views):
            view_copy(d, wrap(mine - d, views), wrap(mine - d, views)).wait_recv()
            for e in range(1, half):
                layer_copy(d, e, me, mate(e)).start()
            pair_copy(d, 0, me).start()
        sum_back(0)
        for d in range(views):
            for e in range(1, half):
                layer_copy(d, e, mate(-e), mate(-e)).wait_recv()
                pair_copy(d, e, mate(-e)).start()
        for d in range(views):
            for e in range(half):
                pair_copy(d, e, mate(-e) + 1 - 2 * side).wait_recv()

    def weigh():
        for d in range(1, views):
            cover_copy(d, d).wait_recv()
        total = cover_part[...]
        for d in range(1, views):
            total = total + cover_in[d]
        cover[...] = RELAXATION / total
        ones = jnp.ones((16, pixels), jnp.bfloat16)
        for slot in range(per_view):
            row_sum = jnp.dot(
                ones, gram[slot * pixels : (slot + 1) * pixels],
                preferred_element_type=jnp.float32,
            )
            defect[slot] = total[slot : slot + 1] - row_sum[:8]

    barrier = pltpu.get_barrier_semaphore()
    for d in range(1, slabs):
        pl.semaphore_signal(
            barrier, inc=1, device_id=slab_device(wrap(me + d, slabs), gz), device_id_type=MESH
        )
    for d in range(1, views):
        pl.semaphore_signal(
            barrier, inc=1, device_id={"view": wrap(mine + d, views)}, device_id_type=MESH
        )

    xs[RIM : RIM + rows] = warm_ref[...]
    xs[ext:] = jnp.zeros((8, pixels), jnp.float32)
    fluxz[:8] = jnp.zeros((8, pixels), jnp.float32)
    zrow = lax.broadcasted_iota(jnp.int32, (ext, RY), 0) + (me * rows - RIM)
    column = lax.broadcasted_iota(jnp.int32, (ext, RY), 1)

    pl.semaphore_wait(barrier, slabs + views - 2)
    for copy in rim_copies(0):
        copy.start()
    for d in range(1, views):
        sum_copy(d).start()
    for d in range(1, views):
        cover_copy(d, d).start()
    take_rims(0)

    def tv_step(step, scale):
        zmask = ((zrow >= 0) & (zrow < depth_total - 1)).astype(jnp.float32)
        cmask = (column < RY - 1).astype(jnp.float32)
        total = jnp.zeros((8, RY), jnp.float32)
        before = None
        here = xs[:ext, :RY]
        for i in range(tiles):
            lanes = slice(i * RY, (i + 1) * RY)
            dz = (xs[1 : ext + 1, lanes] - here) * zmask
            dc = (pltpu.roll(here, RY - 1, 1) - here) * cmask
            square = dz * dz + dc * dc + SMOOTHING
            if i < tiles - 1:
                after = xs[:ext, (i + 1) * RY : (i + 2) * RY]
                di = after - here
                square = square + di * di
            inverse = lax.rsqrt(square)
            fz = dz * inverse
            fc = dc * inverse
            fluxz[8:, lanes] = fz
            g = (fluxz[7 : ext + 7, lanes] - fz) + (pltpu.roll(fc, 1, 1) - fc)
            if before is not None:
                g = g + before
            if i < tiles - 1:
                fi = di * inverse
                g = g - fi
                before = fi
                here = after
            grad[:, lanes] = g
            inner = g[RIM : RIM + rows]
            total = total + jnp.sum((inner * inner).reshape(rows // 8, 8, RY), axis=0)
        own[step] = total
        sends = []
        for d in range(1, slabs):
            copy = pltpu.make_async_remote_copy(
                src_ref=own.at[step],
                dst_ref=stat.at[step, me],
                send_sem=stat_send.at[step, d],
                recv_sem=stat_recv.at[step, d],
                device_id=slab_device(lax.rem(me + d, slabs), gz),
                device_id_type=MESH,
            )
            copy.start()
            sends.append(copy)
        for d in range(1, slabs):
            source = lax.rem(me + slabs - d, slabs)
            pltpu.make_async_remote_copy(
                src_ref=own.at[step],
                dst_ref=stat.at[step, source],
                send_sem=stat_send.at[step, d],
                recv_sem=stat_recv.at[step, d],
                device_id=slab_device(source, gz),
                device_id_type=MESH,
            ).wait_recv()
        for d in range(1, slabs):
            source = lax.rem(me + slabs - d, slabs)
            total = total + stat[step, source]
        for copy in sends:
            copy.wait_send()
        mean = jnp.sum(total, keepdims=True) / (depth_total * pixels)
        factor = scale * lax.rsqrt(mean + NORM_GUARD)
        xs[:ext] = xs[:ext] - factor * grad[...]

    def sart(frame, n):
        x = xs[:ext]
        xb = x.astype(jnp.bfloat16)
        centre = jnp.sum(x, axis=1, keepdims=True) * (1.0 / pixels)
        width = 256
        for lo in range(0, pixels, width):
            lanes = slice(lo, lo + width)
            y = jnp.dot(
                xb, gram[n * pixels : (n + 1) * pixels, lanes], preferred_element_type=jnp.float32
            )
            y = y + centre * defect[n, 0:1, lanes]
            change = (back[frame, n, :, lanes] - y) * cover[n : n + 1, lanes]
            xs[:ext, lanes] = jnp.maximum(x[:, lanes] + change, 0.0)

    def sweep_body(sweep, carry):
        frame = lax.div(sweep, SWEEPS)
        for at in range(1, FRAMES):
            @pl.when(sweep == at * SWEEPS)
            def _():
                for copy in rim_copies(at):
                    copy.start()
                take_rims(at)
                for copy in edge_copies(at):
                    copy.wait_recv()

        for k in range(TV_STEPS):
            scale = jnp.float32(0.0)
            for s in range(SWEEPS):
                value = STEP_SCALE * STEP_DECAY ** (s * TV_STEPS + k)
                scale = jnp.where(lax.rem(sweep, SWEEPS) == s, jnp.float32(value), scale)
            tv_step(sweep * TV_STEPS + k, scale)
            if k == 0:
                @pl.when(sweep == 0)
                def _():
                    sum_gram()

        @pl.when(sweep == 0)
        def _():
            gather_gram()
            spread_edges(0)
            for t in range(1, FRAMES):
                for d in range(1, views):
                    part_copy(t, d).start()
            weigh()
            for copy in edge_copies(0):
                copy.wait_recv()

        for t in range(1, FRAMES):
            @pl.when(sweep == t * SWEEPS - 2)
            def _():
                sum_back(t)

            @pl.when(sweep == t * SWEEPS - 1)
            def _():
                spread_edges(t)

        for n in range(per_view):
            sart(frame, n)

        for t in range(FRAMES):
            @pl.when(sweep == (t + 1) * SWEEPS - 1)
            def _():
                out_ref[t] = xs[RIM : RIM + rows]
        return carry

    lax.fori_loop(0, FRAMES * SWEEPS, sweep_body, 0)

    for d in range(1, views):
        target = wrap(mine + d, views)
        cover_copy(d, d).wait_send()
        sum_copy(d).wait_send()
        view_copy(d, mine, target).wait_send()
        for t in range(FRAMES):
            part_copy(t, d).wait_send()
            full_copy(t, d, mine, target).wait_send()
    for d in range(views):
        for e in range(half):
            if e > 0:
                layer_copy(d, e, me, mate(e)).wait_send()
            pair_copy(d, e, mate(-e)).wait_send()
    for t in range(FRAMES):
        for copy in edge_copies(t):
            copy.wait_send()


def iterate(gram_part, back_part, cover_part, warm, slabs, gz, views):
    rows, pixels = warm.shape
    ext = rows + 2 * RIM
    steps = FRAMES * SWEEPS * TV_STEPS
    per_view = back_part.shape[1]
    piece = gram_part.shape[0] // views
    band = rows // views
    vmem = pl.BlockSpec(memory_space=pltpu.VMEM)
    dma = pltpu.SemaphoreType.DMA
    f32 = jnp.float32
    return pl.pallas_call(
        functools.partial(iterate_kernel, slabs, gz, views),
        out_shape=jax.ShapeDtypeStruct((FRAMES, rows, pixels), f32),
        in_specs=[vmem] * 4,
        out_specs=vmem,
        scratch_shapes=[
            pltpu.VMEM((per_view * pixels, pixels), jnp.bfloat16),
            pltpu.VMEM((views, piece, pixels), jnp.bfloat16),
            pltpu.VMEM((FRAMES, per_view, ext, pixels), f32),
            pltpu.VMEM((FRAMES, views, per_view, band, pixels), f32),
            pltpu.VMEM((views, 8, pixels), f32),
            pltpu.VMEM((8, pixels), f32),
            pltpu.VMEM((ext + 8, pixels), f32),
            pltpu.VMEM((ext, pixels), f32),
            pltpu.VMEM((ext + 8, pixels), f32),
            pltpu.VMEM((per_view, 8, pixels), f32),
            pltpu.VMEM((steps, 8, RY), f32),
            pltpu.VMEM((steps, slabs, 8, RY), f32),
            pltpu.VMEM((FRAMES, 2, RIM, pixels), f32),
            dma((views,)), dma((views,)), dma((views,)), dma((views,)), dma((views,)), dma((views,)),
            dma((views, slabs // 2)), dma((views, slabs // 2)),
            dma((views, slabs // 2)), dma((views, slabs // 2)),
            dma((FRAMES, views)), dma((FRAMES, views)), dma((FRAMES, views)), dma((FRAMES, views)),
            dma((FRAMES, 2)), dma((FRAMES, 2)),
            dma((steps, slabs)), dma((steps, slabs)),
            dma((FRAMES, 2)), dma((FRAMES, 2)),
        ],
        compiler_params=pltpu.CompilerParams(
            collective_id=0, has_side_effects=True, vmem_limit_bytes=40 * 2**20
        ),
    )(gram_part, back_part, cover_part, warm)


def product_kernel(scalars, tile_ref, measured_ref, gram_ref, back_ref, cover_ref, total):
    per_view = scalars.shape[0] - 1
    share = gram_ref.shape[1]
    rows = measured_ref.shape[2]
    pixels, width = tile_ref.shape[1:]
    tile = tile_ref[0]
    ones = jnp.ones((16, pixels), jnp.bfloat16)
    rays = 1.0 / jnp.dot(ones, tile, preferred_element_type=jnp.float32)[0:1]
    first = pl.multiple_of(scalars[per_view] * share, 16)
    parts = [tile_ref[0, pl.ds(first, share), :]]
    parts += [measured_ref[t, 0] for t in range(FRAMES)]
    left = jnp.concatenate(
        [(part.astype(jnp.float32) * rays).astype(jnp.bfloat16) for part in parts]
        + [jnp.ones((16, width), jnp.bfloat16)],
        axis=0,
    )
    step = pl.program_id(1)

    @pl.when(step == 0)
    def _():
        total[...] = jnp.zeros_like(total)

    total[...] += lax.dot_general(
        left, tile, (((1,), (1,)), ((), ())), preferred_element_type=jnp.float32
    )

    @pl.when(step == pl.num_programs(1) - 1)
    def _():
        gram_ref[0] = total[:share].astype(jnp.bfloat16)
        for t in range(FRAMES):
            back_ref[t, 0] = total[share + t * rows : share + (t + 1) * rows]
        cover_ref[0] = total[share + FRAMES * rows :][:8]


def products(scalars, projector, sinogram, slabs):
    per_view, pixels, bins = projector.shape
    rows = sinogram.shape[2]
    share = pixels // slabs
    width = 512 if bins % 512 == 0 else bins
    f32 = jnp.float32
    return pl.pallas_call(
        product_kernel,
        grid_spec=pltpu.PrefetchScalarGridSpec(
            num_scalar_prefetch=1,
            grid=(per_view, bins // width),
            in_specs=[
                pl.BlockSpec((1, pixels, width), lambda n, d, order: (order[n], 0, d)),
                pl.BlockSpec((FRAMES, 1, rows, width), lambda n, d, order: (0, order[n], 0, d)),
            ],
            out_specs=[
                pl.BlockSpec((1, share, pixels), lambda n, d, order: (n, 0, 0)),
                pl.BlockSpec((FRAMES, 1, rows, pixels), lambda n, d, order: (0, n, 0, 0)),
                pl.BlockSpec((1, 8, pixels), lambda n, d, order: (n, 0, 0)),
            ],
            scratch_shapes=[pltpu.VMEM((share + FRAMES * rows + 16, pixels), f32)],
        ),
        out_shape=[
            jax.ShapeDtypeStruct((per_view, share, pixels), jnp.bfloat16),
            jax.ShapeDtypeStruct((FRAMES, per_view, rows, pixels), f32),
            jax.ShapeDtypeStruct((per_view, 8, pixels), f32),
        ],
        compiler_params=pltpu.CompilerParams(
            dimension_semantics=("arbitrary", "arbitrary"), vmem_limit_bytes=32 * 2**20
        ),
    )(scalars, projector, sinogram)


def body(tm, gz, views, sinogram, projector, warm_volume, view_order):
    slices, pixels = warm_volume.shape
    per_view = projector.shape[0]
    slabs = tm * gz
    slab = lax.axis_index("tm") * gz + lax.axis_index("gz")
    scalars = jnp.concatenate([view_order, slab.reshape(1).astype(jnp.int32)])
    gram, back, cover = products(scalars, projector, sinogram, slabs)
    gram = gram.reshape(per_view * (pixels // slabs), pixels)
    cover = jnp.pad(cover[:, 0], ((0, 8 - per_view), (0, 0)), constant_values=1.0)
    return iterate(gram, back, cover, warm_volume, slabs, gz, views)


def solution(mesh):
    return jax.shard_map(
        functools.partial(body, mesh.shape["tm"], mesh.shape["gz"], mesh.shape["view"]),
        mesh=mesh,
        in_specs=(
            P(None, "view", ("tm", "gz"), None),
            P("view", None, None),
            P(("tm", "gz"), None),
            P(),
        ),
        out_specs=P(None, ("tm", "gz"), None),
        check_vma=False,
    )
```

```python
import functools

import jax
import jax.numpy as jnp
from jax import lax
from jax.experimental import pallas as pl
from jax.experimental.pallas import tpu as pltpu
from jax.sharding import PartitionSpec as P

RY = 128
FRAMES = 2
SWEEPS = 3
TV_STEPS = 2
RELAXATION = 0.9
STEP_SCALE = 0.3
STEP_DECAY = 0.7
SMOOTHING = 0.01
NORM_GUARD = 1e-06
RIM = 8

MESH = pl.DeviceIdType.MESH


def slab_device(index, gz):
    return {"tm": lax.div(index, gz), "gz": lax.rem(index, gz)}


def wrap(index, count):
    return lax.rem(index + count, count)


def remote(src, dst, send, recv, device):
    return pltpu.make_async_remote_copy(
        src_ref=src, dst_ref=dst, send_sem=send, recv_sem=recv,
        device_id=device, device_id_type=MESH,
    )


def iterate_kernel(
    slabs, gz, views, gram_part, back_part, cover_part, warm_ref, out_ref,
    gram, gram_in, back, back_in, cover_in, cover, xs, grad, fluxz, defect, own, stat, rim,
    cover_send, cover_recv, sum_send, sum_recv, view_send, view_recv, layer_send, layer_recv,
    pair_send, pair_recv, part_send, part_recv, full_send, full_recv, edge_send, edge_recv,
    stat_send, stat_recv, rim_send, rim_recv,
):
    me = lax.axis_index("tm") * gz + lax.axis_index("gz")
    mine = lax.axis_index("view")
    rows, pixels = warm_ref.shape
    ext = rows + 2 * RIM
    depth_total = slabs * rows
    per_view = gram.shape[0] // pixels
    tiles = pixels // RY
    share = pixels // slabs
    piece = per_view * share // views
    per_slot = views // per_view
    band = rows // views
    half = slabs // 2
    pair = lax.div(me, 2)
    side = lax.rem(me, 2)
    sibling = me + 1 - 2 * side
    up, down = wrap(me + 1, slabs), wrap(me - 1, slabs)

    def gram_rows(slab, view):
        start = lax.div(view, per_slot) * pixels + slab * share + lax.rem(view, per_slot) * piece
        return pl.ds(pl.multiple_of(start, 16), piece)

    def part_rows(view):
        return pl.ds(pl.multiple_of(view * piece, 16), piece)

    def band_rows(view, base):
        return pl.ds(pl.multiple_of(view * band + base, 8), band)

    def rim_copies(at):
        return [
            remote(
                xs.at[pl.ds(source, RIM)], rim.at[at, s],
                rim_send.at[at, s], rim_recv.at[at, s], slab_device(target, gz),
            )
            for s, (source, target) in enumerate(((rows, up), (RIM, down)))
        ]

    def take_rims(at):
        for copy in rim_copies(at):
            copy.wait()
        xs[:RIM] = rim[at, 0]
        xs[RIM + rows : ext] = rim[at, 1]

    def cover_copy(d, to):
        return remote(
            cover_part, cover_in.at[d], cover_send.at[d], cover_recv.at[d],
            {"view": wrap(mine + to, views)},
        )

    def sum_copy(d):
        target = wrap(mine + d, views)
        return remote(
            gram_part.at[part_rows(target)], gram_in.at[d],
            sum_send.at[d], sum_recv.at[d], {"view": target},
        )

    def view_copy(d, view, target):
        at = gram_rows(me, view)
        return remote(
            gram.at[at], gram.at[at], view_send.at[d], view_recv.at[d], {"view": target}
        )

    def layer_copy(d, e, slab, target):
        at = gram_rows(slab, wrap(mine - d, views))
        return remote(
            gram.at[at], gram.at[at], layer_send.at[d, e], layer_recv.at[d, e],
            slab_device(target, gz),
        )

    def mate(e):
        return wrap(pair + e, half) * 2 + side

    def pair_copy(d, e, slab):
        at = gram_rows(slab, wrap(mine - d, views))
        return remote(
            gram.at[at], gram.at[at], pair_send.at[d, e], pair_recv.at[d, e],
            slab_device(sibling, gz),
        )

    def part_copy(t, d):
        target = wrap(mine + d, views)
        return remote(
            back_part.at[t, :, band_rows(target, 0)], back_in.at[t, d],
            part_send.at[t, d], part_recv.at[t, d], {"view": target},
        )

    def full_copy(t, d, view, target):
        at = back.at[t, :, band_rows(view, RIM)]
        return remote(at, at, full_send.at[t, d], full_recv.at[t, d], {"view": target})

    def edge_copies(t):
        return [
            remote(
                back.at[t, :, pl.ds(source, RIM)], back.at[t, :, pl.ds(dest, RIM)],
                edge_send.at[t, s], edge_recv.at[t, s], slab_device(target, gz),
            )
            for s, (source, dest, target) in enumerate(
                ((rows, 0, up), (RIM, rows + RIM, down))
            )
        ]

    def sum_back(t):
        total = back_part[t, :, band_rows(mine, 0)]
        for d in range(1, views):
            part_copy(t, d).wait_recv()
            total = total + back_in[t, d]
        back[t, :, band_rows(mine, RIM)] = total
        for d in range(1, views):
            full_copy(t, d, mine, wrap(mine + d, views)).start()

    def spread_edges(t):
        for d in range(1, views):
            full_copy(t, d, wrap(mine - d, views), wrap(mine - d, views)).wait_recv()
        for copy in edge_copies(t):
            copy.start()

    def sum_gram():
        total = gram_part[part_rows(mine)].astype(jnp.float32)
        for d in range(1, views):
            sum_copy(d).wait_recv()
            total = total + gram_in[d].astype(jnp.float32)
        gram[gram_rows(me, mine)] = total.astype(jnp.bfloat16)
        for d in range(1, views):
            view_copy(d, mine, wrap(mine + d, views)).start()
        for e in range(1, half):
            layer_copy(0, e, me, mate(e)).start()
        pair_copy(0, 0, me).start()
        for d in range(1, views):
            part_copy(0, d).start()

    def gather_gram():
        for d in range(1, views):
            view_copy(d, wrap(mine - d, views), wrap(mine - d, views)).wait_recv()
            for e in range(1, half):
                layer_copy(d, e, me, mate(e)).start()
            pair_copy(d, 0, me).start()
        sum_back(0)
        for d in range(views):
            for e in range(1, half):
                layer_copy(d, e, mate(-e), mate(-e)).wait_recv()
                pair_copy(d, e, mate(-e)).start()
        for d in range(views):
            for e in range(half):
                pair_copy(d, e, mate(-e) + 1 - 2 * side).wait_recv()

    def weigh():
        for d in range(1, views):
            cover_copy(d, d).wait_recv()
        total = cover_part[...]
        for d in range(1, views):
            total = total + cover_in[d]
        cover[...] = RELAXATION / total
        ones = jnp.ones((16, pixels), jnp.bfloat16)
        for slot in range(per_view):
            row_sum = jnp.dot(
                ones, gram[slot * pixels : (slot + 1) * pixels],
                preferred_element_type=jnp.float32,
            )
            defect[slot] = total[slot : slot + 1] - row_sum[:8]

    barrier = pltpu.get_barrier_semaphore()
    for d in range(1, slabs):
        pl.semaphore_signal(
            barrier, inc=1, device_id=slab_device(wrap(me + d, slabs), gz), device_id_type=MESH
        )
    for d in range(1, views):
        pl.semaphore_signal(
            barrier, inc=1, device_id={"view": wrap(mine + d, views)}, device_id_type=MESH
        )

    xs[RIM : RIM + rows] = warm_ref[...]
    xs[ext:] = jnp.zeros((8, pixels), jnp.float32)
    fluxz[:8] = jnp.zeros((8, pixels), jnp.float32)
    zrow = lax.broadcasted_iota(jnp.int32, (ext, RY), 0) + (me * rows - RIM)
    column = lax.broadcasted_iota(jnp.int32, (ext, RY), 1)

    pl.semaphore_wait(barrier, slabs + views - 2)
    for copy in rim_copies(0):
        copy.start()
    for d in range(1, views):
        sum_copy(d).start()
    for d in range(1, views):
        cover_copy(d, d).start()
    take_rims(0)

    def tv_step(step, scale):
        zmask = ((zrow >= 0) & (zrow < depth_total - 1)).astype(jnp.float32)
        cmask = (column < RY - 1).astype(jnp.float32)
        total = jnp.zeros((8, RY), jnp.float32)
        before = None
        here = xs[:ext, :RY]
        for i in range(tiles):
            lanes = slice(i * RY, (i + 1) * RY)
            dz = (xs[1 : ext + 1, lanes] - here) * zmask
            dc = (pltpu.roll(here, RY - 1, 1) - here) * cmask
            square = dz * dz + dc * dc + SMOOTHING
            if i < tiles - 1:
                after = xs[:ext, (i + 1) * RY : (i + 2) * RY]
                di = after - here
                square = square + di * di
            inverse = lax.rsqrt(square)
            fz = dz * inverse
            fc = dc * inverse
            fluxz[8:, lanes] = fz
            g = (fluxz[7 : ext + 7, lanes] - fz) + (pltpu.roll(fc, 1, 1) - fc)
            if before is not None:
                g = g + before
            if i < tiles - 1:
                fi = di * inverse
                g = g - fi
                before = fi
                here = after
            grad[:, lanes] = g
            inner = g[RIM : RIM + rows]
            total = total + jnp.sum((inner * inner).reshape(rows // 8, 8, RY), axis=0)
        own[step] = total
        sends = []
        for d in range(1, slabs):
            copy = pltpu.make_async_remote_copy(
                src_ref=own.at[step],
                dst_ref=stat.at[step, me],
                send_sem=stat_send.at[step, d],
                recv_sem=stat_recv.at[step, d],
                device_id=slab_device(lax.rem(me + d, slabs), gz),
                device_id_type=MESH,
            )
            copy.start()
            sends.append(copy)
        for d in range(1, slabs):
            source = lax.rem(me + slabs - d, slabs)
            pltpu.make_async_remote_copy(
                src_ref=own.at[step],
                dst_ref=stat.at[step, source],
                send_sem=stat_send.at[step, d],
                recv_sem=stat_recv.at[step, d],
                device_id=slab_device(source, gz),
                device_id_type=MESH,
            ).wait_recv()
        for d in range(1, slabs):
            source = lax.rem(me + slabs - d, slabs)
            total = total + stat[step, source]
        for copy in sends:
            copy.wait_send()
        mean = jnp.sum(total, keepdims=True) / (depth_total * pixels)
        factor = scale * lax.rsqrt(mean + NORM_GUARD)
        xs[:ext] = xs[:ext] - factor * grad[...]

    def sart(frame, n):
        x = xs[:ext]
        xb = x.astype(jnp.bfloat16)
        centre = jnp.sum(x, axis=1, keepdims=True) * (1.0 / pixels)
        width = 256
        for lo in range(0, pixels, width):
            lanes = slice(lo, lo + width)
            y = jnp.dot(
                xb, gram[n * pixels : (n + 1) * pixels, lanes], preferred_element_type=jnp.float32
            )
            y = y + centre * defect[n, 0:1, lanes]
            change = (back[frame, n, :, lanes] - y) * cover[n : n + 1, lanes]
            xs[:ext, lanes] = jnp.maximum(x[:, lanes] + change, 0.0)

    def sweep_body(sweep, carry):
        frame = lax.div(sweep, SWEEPS)
        for at in range(1, FRAMES):
            @pl.when(sweep == at * SWEEPS)
            def _():
                for copy in rim_copies(at):
                    copy.start()
                take_rims(at)
                for copy in edge_copies(at):
                    copy.wait_recv()

        for k in range(TV_STEPS):
            scale = jnp.float32(0.0)
            for s in range(SWEEPS):
                value = STEP_SCALE * STEP_DECAY ** (s * TV_STEPS + k)
                scale = jnp.where(lax.rem(sweep, SWEEPS) == s, jnp.float32(value), scale)
            tv_step(sweep * TV_STEPS + k, scale)
            if k == 0:
                @pl.when(sweep == 0)
                def _():
                    sum_gram()

        @pl.when(sweep == 0)
        def _():
            gather_gram()
            spread_edges(0)
            for t in range(1, FRAMES):
                for d in range(1, views):
                    part_copy(t, d).start()
            weigh()
            for copy in edge_copies(0):
                copy.wait_recv()

        for t in range(1, FRAMES):
            @pl.when(sweep == t * SWEEPS - 2)
            def _():
                sum_back(t)

            @pl.when(sweep == t * SWEEPS - 1)
            def _():
                spread_edges(t)

        for n in range(per_view):
            sart(frame, n)

        for t in range(FRAMES):
            @pl.when(sweep == (t + 1) * SWEEPS - 1)
            def _():
                out_ref[t] = xs[RIM : RIM + rows]
        return carry

    lax.fori_loop(0, FRAMES * SWEEPS, sweep_body, 0)

    for d in range(1, views):
        target = wrap(mine + d, views)
        cover_copy(d, d).wait_send()
        sum_copy(d).wait_send()
        view_copy(d, mine, target).wait_send()
        for t in range(FRAMES):
            part_copy(t, d).wait_send()
            full_copy(t, d, mine, target).wait_send()
    for d in range(views):
        for e in range(half):
            if e > 0:
                layer_copy(d, e, me, mate(e)).wait_send()
            pair_copy(d, e, mate(-e)).wait_send()
    for t in range(FRAMES):
        for copy in edge_copies(t):
            copy.wait_send()


def iterate(gram_part, back_part, cover_part, warm, slabs, gz, views):
    rows, pixels = warm.shape
    ext = rows + 2 * RIM
    steps = FRAMES * SWEEPS * TV_STEPS
    per_view = back_part.shape[1]
    piece = gram_part.shape[0] // views
    band = rows // views
    vmem = pl.BlockSpec(memory_space=pltpu.VMEM)
    dma = pltpu.SemaphoreType.DMA
    f32 = jnp.float32
    return pl.pallas_call(
        functools.partial(iterate_kernel, slabs, gz, views),
        out_shape=jax.ShapeDtypeStruct((FRAMES, rows, pixels), f32),
        in_specs=[vmem] * 4,
        out_specs=vmem,
        scratch_shapes=[
            pltpu.VMEM((per_view * pixels, pixels), jnp.bfloat16),
            pltpu.VMEM((views, piece, pixels), jnp.bfloat16),
            pltpu.VMEM((FRAMES, per_view, ext, pixels), f32),
            pltpu.VMEM((FRAMES, views, per_view, band, pixels), f32),
            pltpu.VMEM((views, 8, pixels), f32),
            pltpu.VMEM((8, pixels), f32),
            pltpu.VMEM((ext + 8, pixels), f32),
            pltpu.VMEM((ext, pixels), f32),
            pltpu.VMEM((ext + 8, pixels), f32),
            pltpu.VMEM((per_view, 8, pixels), f32),
            pltpu.VMEM((steps, 8, RY), f32),
            pltpu.VMEM((steps, slabs, 8, RY), f32),
            pltpu.VMEM((FRAMES, 2, RIM, pixels), f32),
            dma((views,)), dma((views,)), dma((views,)), dma((views,)), dma((views,)), dma((views,)),
            dma((views, slabs // 2)), dma((views, slabs // 2)),
            dma((views, slabs // 2)), dma((views, slabs // 2)),
            dma((FRAMES, views)), dma((FRAMES, views)), dma((FRAMES, views)), dma((FRAMES, views)),
            dma((FRAMES, 2)), dma((FRAMES, 2)),
            dma((steps, slabs)), dma((steps, slabs)),
            dma((FRAMES, 2)), dma((FRAMES, 2)),
        ],
        compiler_params=pltpu.CompilerParams(
            collective_id=0, has_side_effects=True, vmem_limit_bytes=40 * 2**20
        ),
    )(gram_part, back_part, cover_part, warm)


def product_kernel(scalars, tile_ref, measured_ref, gram_ref, back_ref, cover_ref, total):
    per_view = scalars.shape[0] - 1
    share = gram_ref.shape[1]
    rows = measured_ref.shape[2]
    pixels, width = tile_ref.shape[1:]
    tile = tile_ref[0]
    ones = jnp.ones((16, pixels), jnp.bfloat16)
    rays = 1.0 / jnp.dot(ones, tile, preferred_element_type=jnp.float32)[0:1]
    first = pl.multiple_of(scalars[per_view] * share, 16)
    parts = [tile_ref[0, pl.ds(first, share), :]]
    parts += [measured_ref[t, 0] for t in range(FRAMES)]
    left = jnp.concatenate(
        [(part.astype(jnp.float32) * rays).astype(jnp.bfloat16) for part in parts]
        + [jnp.ones((16, width), jnp.bfloat16)],
        axis=0,
    )
    step = pl.program_id(1)

    @pl.when(step == 0)
    def _():
        total[...] = jnp.zeros_like(total)

    total[...] += lax.dot_general(
        left, tile, (((1,), (1,)), ((), ())), preferred_element_type=jnp.float32
    )

    @pl.when(step == pl.num_programs(1) - 1)
    def _():
        gram_ref[0] = total[:share].astype(jnp.bfloat16)
        for t in range(FRAMES):
            back_ref[t, 0] = total[share + t * rows : share + (t + 1) * rows]
        cover_ref[0] = total[share + FRAMES * rows :][:8]


def products(scalars, projector, sinogram, slabs):
    per_view, pixels, bins = projector.shape
    rows = sinogram.shape[2]
    share = pixels // slabs
    width = 512 if bins % 512 == 0 else bins
    f32 = jnp.float32
    return pl.pallas_call(
        product_kernel,
        grid_spec=pltpu.PrefetchScalarGridSpec(
            num_scalar_prefetch=1,
            grid=(per_view, bins // width),
            in_specs=[
                pl.BlockSpec((1, pixels, width), lambda n, d, order: (order[n], 0, d)),
                pl.BlockSpec((FRAMES, 1, rows, width), lambda n, d, order: (0, order[n], 0, d)),
            ],
            out_specs=[
                pl.BlockSpec((1, share, pixels), lambda n, d, order: (n, 0, 0)),
                pl.BlockSpec((FRAMES, 1, rows, pixels), lambda n, d, order: (0, n, 0, 0)),
                pl.BlockSpec((1, 8, pixels), lambda n, d, order: (n, 0, 0)),
            ],
            scratch_shapes=[pltpu.VMEM((share + FRAMES * rows + 16, pixels), f32)],
        ),
        out_shape=[
            jax.ShapeDtypeStruct((per_view, share, pixels), jnp.bfloat16),
            jax.ShapeDtypeStruct((FRAMES, per_view, rows, pixels), f32),
            jax.ShapeDtypeStruct((per_view, 8, pixels), f32),
        ],
        compiler_params=pltpu.CompilerParams(
            dimension_semantics=("arbitrary", "arbitrary"), vmem_limit_bytes=58 * 2**20
        ),
    )(scalars, projector, sinogram)


def body(tm, gz, views, sinogram, projector, warm_volume, view_order):
    slices, pixels = warm_volume.shape
    per_view = projector.shape[0]
    slabs = tm * gz
    slab = lax.axis_index("tm") * gz + lax.axis_index("gz")
    scalars = jnp.concatenate([view_order, slab.reshape(1).astype(jnp.int32)])
    gram, back, cover = products(scalars, projector, sinogram, slabs)
    gram = gram.reshape(per_view * (pixels // slabs), pixels)
    cover = jnp.pad(cover[:, 0], ((0, 8 - per_view), (0, 0)), constant_values=1.0)
    return iterate(gram, back, cover, warm_volume, slabs, gz, views)


def solution(mesh):
    return jax.shard_map(
        functools.partial(body, mesh.shape["tm"], mesh.shape["gz"], mesh.shape["view"]),
        mesh=mesh,
        in_specs=(
            P(None, "view", ("tm", "gz"), None),
            P("view", None, None),
            P(("tm", "gz"), None),
            P(),
        ),
        out_specs=P(None, ("tm", "gz"), None),
        check_vma=False,
    )
```
